32 devices in a mesh: groups: 2 (over y), adapter: 4 (over z), tensor: 2 (over x), dp: 2 (over core).
Axes of the slice: x: 2, y: 2, z: 4, core: 2. Of those that a mesh axis runs over, the one named last changes fastest.
Arguments:
- tokens: bfloat16 [4096, 8192], P(('groups', 'adapter', 'dp'), 'tensor'), parts along dimension 0, may hold values from -6 to 6
- frozen_value_weight: bfloat16 [8192, 1024], P('tensor'), may hold values from -0.0625 to 0.0625
- adapter_down_weight: bfloat16 [128, 16, 8192], P(('groups', 'adapter'), None, 'tensor'), parts along dimension 0, may hold values from -0.0625 to 0.0625
- adapter_up_weight: bfloat16 [128, 16, 1024], P(('groups', 'adapter'), None, 'tensor'), parts along dimension 0, may hold values from -0.1875 to 0.1875
- token_adapter: int32 [4096], P(('groups', 'adapter', 'dp')), parts along dimension 0, may hold values from 0 to 63, as said below
- adapter_storage_row: int32 [128], P('groups'), parts along dimension 0, may hold values from 0 to 63, as said below
- upstream: bfloat16 [4096, 1024], P(('groups', 'adapter', 'dp'), 'tensor'), parts along dimension 0, may hold values from -6 to 6
Outputs:
- projected: bfloat16 [4096, 1024], P(('groups', 'adapter', 'dp'), 'tensor'), parts along dimension 0
- token_input_gradient: bfloat16 [4096, 8192], P(('groups', 'adapter', 'dp'), 'tensor'), parts along dimension 0
- grad_down: float32 [128, 16, 8192], P(('groups', 'adapter'), None, 'tensor'), parts along dimension 0
- grad_up: float32 [128, 16, 1024], P(('groups', 'adapter'), None, 'tensor'), parts along dimension 0
The draws below stay inside these ranges and needn't reach their ends.
There are 2 independent parts, one for each index of `groups`. The reference program is written for one: setup_inputs(seed, part) draws one part's arguments, and reference() takes and returns one part's arrays. A program takes and returns all parts, laid end to end along the dimension named above; an argument that names none is the same for every part. Nothing has to cross between parts.
Inputs may be any that keep to these rules, and one draw needn't show every extreme that they name: A token's adapter is owned by index adapter_storage_row[token_adapter] // 16 of adapter. Of the 256 tokens of one device (aligned blocks of the token dimension), exactly 192 belong to one owner, the same owner for every device of one part; every other owner gets at most 22 of them, and some owner exactly 22. `adapter_storage_row`: A permutation.
All inputs are finite; a program needn't handle non-finite values.
Results may differ from the reference program's by a relative error of at most 0.0034.
Values may be sent and summed in bfloat16 or wider, within the bound.
A program may use at most 128 MiB of HBM per device.

```python
import jax
import jax.numpy as jnp
from jax import lax

MODEL_WIDTH = 8192
ADAPTER_RANK = 16
ADP_DEV = 16
TOK_DEV = 256
VALUE_WIDTH = 1024
ADAPTER_TOTAL = 64
TOKEN_TOTAL = 2048
CAP = 192
N_ADAPTER = 4


def shuffle_row(row_key, row):
    return jax.random.permutation(row_key, row)


def shared_routes(key):
    key_map, key_hot, key_shift, key_shuffle, key_slot = jax.random.split(key, 5)
    adapter_storage_row = jax.random.permutation(key_map, ADAPTER_TOTAL).astype(jnp.int32)
    hottest = jax.random.randint(key_hot, (), 0, N_ADAPTER)
    blocks = TOKEN_TOTAL // TOK_DEV
    shifts = jax.random.randint(key_shift, (blocks, 1), 0, N_ADAPTER - 1)
    order = jnp.arange(TOK_DEV, dtype=jnp.int32)[None, :]
    others = 1 + (order - CAP + shifts) % (N_ADAPTER - 1)
    relative = jnp.where(order < CAP, 0, others)
    owner_of = (hottest + relative) % N_ADAPTER
    shuffle_keys = jax.random.split(key_shuffle, blocks)
    owner_of = jax.vmap(shuffle_row)(shuffle_keys, owner_of)
    local_slot = jax.random.randint(key_slot, (blocks, TOK_DEV), 0, ADP_DEV)
    storage = (owner_of * ADP_DEV + local_slot).reshape(-1)
    inverse = jnp.zeros((ADAPTER_TOTAL,), jnp.int32).at[adapter_storage_row].set(jnp.arange(ADAPTER_TOTAL, dtype=jnp.int32))
    return (inverse[storage].astype(jnp.int32), adapter_storage_row)


def draw_token_adapter(key, part):
    routes = shared_routes(key)
    return routes[0]


def draw_adapter_storage_row(key, part):
    routes = shared_routes(key)
    return routes[1]


def level_of(own_key, dims, pieces, low, largest):
    def one(dim, blocks):
        heights = jax.random.uniform(jax.random.fold_in(jax.random.fold_in(own_key, 6), dim), (blocks,), jnp.float32, low / len(pieces), largest / len(pieces))
        return jnp.repeat(jnp.exp(heights), dims[dim] // blocks).reshape((-1,) + (1,) * (len(dims) - dim - 1))

    gain = one(*pieces[0])
    for cut in pieces[1:]:
        gain = gain * one(*cut)
    return gain


def scatter_about(rng, shape, width, most, shards=(), kind=jnp.bfloat16):
    level = level_of(rng, shape, shards, -0.22, 0.18) if shards else 1.0
    array = jax.random.normal(rng, shape, jnp.float32) * width * level
    return jnp.minimum(jnp.maximum(array, -most), most).astype(kind)


def setup_inputs(seed: int = 0, part: int = 0) -> dict:
    key_list = jax.random.split(jax.random.key(seed), 8)
    part_keys = jax.random.split(jax.random.fold_in(key_list[7], part), 8)
    return {
        "tokens": scatter_about(part_keys[0], (TOKEN_TOTAL, MODEL_WIDTH), 1.0, 6.0, ((0, 8), (1, 2))),
        "frozen_value_weight": scatter_about(key_list[1], (MODEL_WIDTH, VALUE_WIDTH), MODEL_WIDTH ** -0.5, 0.0625, ((0, 2),)),
        "adapter_down_weight": scatter_about(part_keys[2], (ADAPTER_TOTAL, ADAPTER_RANK, MODEL_WIDTH), MODEL_WIDTH ** -0.5, 0.0625, ((0, 4), (2, 2))),
        "adapter_up_weight": scatter_about(part_keys[3], (ADAPTER_TOTAL, ADAPTER_RANK, VALUE_WIDTH), VALUE_WIDTH ** -0.5, 0.1875, ((0, 4), (2, 2))),
        "token_adapter": draw_token_adapter(jax.random.fold_in(jax.random.fold_in(key_list[7], part), 71), part),
        "adapter_storage_row": draw_adapter_storage_row(jax.random.fold_in(jax.random.fold_in(key_list[7], part), 71), part),
        "upstream": scatter_about(part_keys[6], (TOKEN_TOTAL, VALUE_WIDTH), 1.0, 6.0, ((0, 8), (1, 2))),
    }


adapter_scale = 2.0


def reference(tokens, frozen_value_weight, adapter_down_weight, adapter_up_weight, token_adapter, adapter_storage_row, upstream):
    storage = adapter_storage_row[token_adapter].astype(jnp.int32)
    frozen_output = jnp.dot(tokens, frozen_value_weight, preferred_element_type=jnp.float32)
    frozen_backward = lax.dot_general(upstream, frozen_value_weight, (((1,), (1,)), ((), ())), preferred_element_type=jnp.float32)
    blocks = TOKEN_TOTAL // TOK_DEV
    entry_list = (tokens.reshape(blocks, TOK_DEV, MODEL_WIDTH), upstream.reshape(blocks, TOK_DEV, VALUE_WIDTH), storage.reshape(blocks, TOK_DEV))

    def block_stride(carry, item):
        down_gradient_sum, up_gradient_sum = carry
        rows, upper, storage_positions = item
        down_matrix_rows = adapter_down_weight[storage_positions].astype(jnp.float32)
        up_matrix_rows = adapter_up_weight[storage_positions].astype(jnp.float32)
        rank_activation = jnp.einsum("td,trd->tr", rows.astype(jnp.float32), down_matrix_rows).astype(jnp.bfloat16)
        adapter_output = (adapter_scale * jnp.einsum("cz,czh->ch", rank_activation.astype(jnp.float32), up_matrix_rows)).astype(jnp.bfloat16)
        backward_rows = jnp.einsum("tk,trk->tr", upper.astype(jnp.float32), up_matrix_rows).astype(jnp.bfloat16)
        adapter_backward = (adapter_scale * jnp.einsum("qe,qeb->qb", backward_rows.astype(jnp.float32), down_matrix_rows)).astype(jnp.bfloat16)
        down_gradient_sum = down_gradient_sum.at[storage_positions].add(jnp.einsum("tr,td->trd", backward_rows.astype(jnp.float32), rows.astype(jnp.float32)))
        up_gradient_sum = up_gradient_sum.at[storage_positions].add(jnp.einsum("tr,tk->trk", rank_activation.astype(jnp.float32), upper.astype(jnp.float32)))
        return (down_gradient_sum, up_gradient_sum), (adapter_output, adapter_backward)

    offset_begin = (jnp.zeros((ADAPTER_TOTAL, ADAPTER_RANK, MODEL_WIDTH), jnp.float32), jnp.zeros((ADAPTER_TOTAL, ADAPTER_RANK, VALUE_WIDTH), jnp.float32))
    (down_gradient_sum, up_gradient_sum), (adapter_output, adapter_backward) = lax.scan(block_stride, offset_begin, entry_list)
    projected = (frozen_output + adapter_output.reshape(TOKEN_TOTAL, VALUE_WIDTH).astype(jnp.float32)).astype(jnp.bfloat16)
    token_input_gradient = (frozen_backward + adapter_backward.reshape(TOKEN_TOTAL, MODEL_WIDTH).astype(jnp.float32)).astype(jnp.bfloat16)
    return projected, token_input_gradient, adapter_scale * down_gradient_sum, adapter_scale * up_gradient_sum
```

```python
import jax
import jax.numpy as jnp
from jax import lax
from jax.experimental import pallas as pl
from jax.experimental.pallas import tpu as pltpu
from jax.sharding import PartitionSpec as P

MESH = pl.DeviceIdType.MESH
F32 = jnp.float32
BF16 = jnp.bfloat16
SCALE = 2.0
CHUNKS = 8
SMALL_CHUNKS = 2


def dot(a, b):
    return lax.dot_general(a, b, (((1,), (0,)), ((), ())), preferred_element_type=F32)


def dot_nt(a, b):
    return lax.dot_general(a, b, (((1,), (1,)), ((), ())), preferred_element_type=F32)


def tiled(total, tile, body):
    tile = min(tile, total)

    def step(i, carry):
        body(pl.ds(pl.multiple_of(i * tile, tile), tile))
        return carry

    lax.fori_loop(0, total // tile, step, 0)


def make_kernel(n, nx, nc, ranks, slots, planes):
    def kernel(
        ta_ref, asr_ref, tok_ref, w_hbm, a_ref, b_ref, u_ref,
        proj_ref, dxo_ref, gd_ref, gu_ref,
        w_ref, ta2, tok2, u2, ufull, basep, baser, fb,
        pack_m, mask_h, mask_r, spread_s, spread_t,
        send_t, recv_t, send_u, recv_u, ret_t, back_t, ret_u, back_u,
        rb_hot, rl_hot, rr,
        b_r, b_l, b_sr, b_sl, bh,
        c_r, c_l, c_sr, c_sl, g_hot, ah,
        v_r, v_l, v_sr, v_sl, gv_hot,
        dx2, dxs, lo2, los,
        wsem, lsem, sib_s, sib_r, ux_s, ux_r, bs_s, bs_r, rk_s, rk_r, aa_s, aa_r,
        bc_s, bc_r, cc_s, cc_r, vc_s, vc_r,
    ):
        td, d = tok_ref.shape
        er = a_ref.shape[0]
        e_local = er // ranks
        vl = u_ref.shape[1]
        v = w_ref.shape[1]
        dh, vh = d // nc, vl // nc
        t2 = nc * td
        ns = n * slots
        z, x, c = lax.axis_index("adapter"), lax.axis_index("tensor"), lax.axis_index("dp")
        sib = lax.rem(c + 1, nc)
        me_xc = x * nc + c
        my_cols = pl.ds(pl.multiple_of(c * dh, dh), dh)
        sib_cols = pl.ds(pl.multiple_of(sib * dh, dh), dh)
        my_vcols = pl.ds(pl.multiple_of(c * vh, vh), vh)
        sib_vcols = pl.ds(pl.multiple_of(sib * vh, vh), vh)
        my_rows = pl.ds(pl.multiple_of(c * td, td), td)
        sib_rows = pl.ds(pl.multiple_of(sib * td, td), td)

        w_copy = pltpu.make_async_copy(w_hbm, w_ref, wsem)
        w_copy.start()

        xc_peers = []
        for j in range(1, nx * nc):
            o = lax.rem(me_xc + j, nx * nc)
            xc_peers.append((o, o // nc, o % nc))
        z_peers = [lax.rem(z + j, n) for j in range(1, n)]
        x_peers = [lax.rem(x + j, nx) for j in range(1, nx)]

        barrier = pltpu.get_barrier_semaphore()
        for _, px, pc in xc_peers:
            pl.semaphore_signal(barrier, inc=1, device_id={"tensor": px, "dp": pc}, device_id_type=MESH)
        for pz in z_peers:
            pl.semaphore_signal(barrier, inc=1, device_id={"adapter": pz}, device_id_type=MESH)
        pl.semaphore_wait(barrier, len(xc_peers) + len(z_peers))

        def sib_copy(k, src, dst):
            return pltpu.make_async_remote_copy(
                src, dst, sib_s.at[k], sib_r.at[k], device_id={"dp": sib}, device_id_type=MESH
            )

        def z_copy(k, src, dst, to, frm):
            return pltpu.make_async_remote_copy(
                src, dst, aa_s.at[k, to], aa_r.at[k, frm], device_id={"adapter": to}, device_id_type=MESH
            )

        ta_c = sib_copy(0, ta_ref, ta2.at[c])
        tok_c = sib_copy(1, tok_ref.at[:, sib_cols], tok2.at[my_rows])
        u_c = sib_copy(2, u_ref.at[:, sib_vcols], u2.at[my_rows])
        ta_c.start()
        u_c.start()
        tok_c.start()
        for px in x_peers:
            pltpu.make_async_remote_copy(
                u_ref, ufull.at[x], ux_s.at[px], ux_r.at[x], device_id={"tensor": px}, device_id_type=MESH
            ).start()
        tok_l = pltpu.make_async_copy(tok_ref.at[:, my_cols], tok2.at[my_rows_of(c, td)], lsem.at[0])
        u_l = pltpu.make_async_copy(u_ref.at[:, my_vcols], u2.at[my_rows_of(c, td)], lsem.at[1])
        tok_l.start()
        u_l.start()
        ta2[c] = ta_ref[...]
        ufull[x] = u_ref[...]

        ta_c.wait_recv()
        ids = jnp.concatenate([ta2[i] for i in range(nc)], axis=1)
        at = asr_ref.shape[1]
        match = (lax.broadcasted_iota(jnp.int32, (at, t2), 0) == ids).astype(F32).astype(BF16)
        table = jnp.broadcast_to(asr_ref[...].astype(F32), (8, at)).astype(BF16)
        storage = dot(table, match)[0:1, :]
        owner = jnp.floor(storage * (1.0 / e_local))
        slot = storage - owner * e_local
        n8 = max(8, n)
        own_iota = lax.broadcasted_iota(jnp.int32, (n8, t2), 0).astype(F32)
        own_hit = jnp.where(own_iota == owner, 1.0, 0.0)
        loads = jnp.sum(own_hit, axis=1, keepdims=True)
        top = jnp.max(loads)
        hot = jnp.sum(jnp.where(loads == top, lax.broadcasted_iota(jnp.int32, (n8, 1), 0).astype(F32), 0.0))
        zf = z.astype(F32)
        w_is = jnp.where(hot == zf, 1.0, 0.0)
        w_lt = jnp.where(hot < zf, 1.0, 0.0)
        w_gt = jnp.where(hot > zf, 1.0, 0.0)
        tri = (
            lax.broadcasted_iota(jnp.int32, (t2, t2), 0) < lax.broadcasted_iota(jnp.int32, (t2, t2), 1)
        ).astype(F32).astype(BF16)
        pos = jnp.sum(dot(own_hit.astype(BF16), tri) * own_hit, axis=0, keepdims=True)
        target = jnp.where(owner == hot, -1.0, owner * slots + pos)
        pack_m[...] = jnp.where(
            lax.broadcasted_iota(jnp.int32, (ns, t2), 0).astype(F32) == target, 1.0, 0.0
        ).astype(BF16)
        begin = jnp.where(owner == hot, slot * ranks, -1.0 * ranks)
        er_iota = lax.broadcasted_iota(jnp.int32, (er, t2), 0).astype(F32)
        mask_h[...] = jnp.where(er_iota >= begin, 1.0, 0.0) * jnp.where(er_iota < begin + ranks, 1.0, 0.0)
        slot_hit = jnp.where(
            lax.broadcasted_iota(jnp.int32, (128, t2), 0).astype(F32) == slot, 1.0, 0.0
        ).astype(BF16)

        def clear_edges(right, left):
            @pl.when(z == 0)
            def _():
                right[...] = jnp.zeros_like(right)

            @pl.when(z == n - 1)
            def _():
                left[...] = jnp.zeros_like(left)

        def load(ref, rows):
            total = ref[0, rows, :].astype(F32)
            for p in range(1, planes):
                total += ref[p, rows, :].astype(F32)
            return total

        def store(ref, rows, value):
            for p in range(planes):
                part = value.astype(BF16)
                ref[p, rows, :] = part
                value = value - part.astype(F32)

        def chain_copy(src, dst, ssem, rsem, way, k, rows, to):
            return [
                pltpu.make_async_remote_copy(
                    src.at[p, rows], dst.at[p, rows], ssem.at[way, p, k], rsem.at[way, p, k],
                    device_id={"adapter": to}, device_id_type=MESH,
                )
                for p in range(planes)
            ]

        def chain_step(s, chunks, rr_, rl_, sr_, sl_, ssem, rsem, value):
            rc = er // chunks
            for way, (rin, sout, lag, edge_in, edge_out, step) in enumerate((
                (rr_, sr_, z, z == 0, z == n - 1, 1),
                (rl_, sl_, n - 1 - z, z == n - 1, z == 0, -1),
            )):
                k = s - lag

                @pl.when(jnp.logical_and(k >= 0, k < chunks))
                def _():
                    rows = pl.ds(pl.multiple_of(k * rc, rc), rc)
                    to = lax.rem(z + step + n, n)

                    @pl.when(jnp.logical_not(edge_in))
                    def _():
                        for cp in chain_copy(sout, rin, ssem, rsem, way, k, rows, to):
                            cp.wait_recv()

                    @pl.when(jnp.logical_not(edge_out))
                    def _():
                        store(sout, rows, value(way, rows, load(rin, rows)))
                        for cp in chain_copy(sout, rin, ssem, rsem, way, k, rows, to):
                            cp.start()

        def chain_finish(chunks, rr_, rl_, sr_, sl_, ssem, rsem):
            rc = er // chunks
            for way, (rin, sout, edge_out, step) in enumerate(
                ((rr_, sr_, z == n - 1, 1), (rl_, sl_, z == 0, -1))
            ):
                to = lax.rem(z + step + n, n)

                @pl.when(jnp.logical_not(edge_out))
                def _():
                    for k in range(chunks):
                        for cp in chain_copy(sout, rin, ssem, rsem, way, k, pl.ds(k * rc, rc), to):
                            cp.wait_send()

        clear_edges(b_r, b_l)
        clear_edges(c_r, c_l)
        clear_edges(v_r, v_l)

        b_args = (SMALL_CHUNKS, b_r, b_l, b_sr, b_sl, bc_s, bc_r)

        def b_value(way, rows, got):
            return w_is * b_ref[rows, my_vcols].astype(F32) + (1.0 - w_is) * got

        b_steps = SMALL_CHUNKS + n - 1
        chain_step(0, *b_args, b_value)
        tok_l.wait()
        u_l.wait()
        u_c.wait_recv()
        send_u[:, 0:vh] = dot(pack_m[...], u2[...]).astype(BF16)
        send_u[:, vh : vh + 128] = dot_nt(pack_m[...], slot_hit).astype(BF16)
        for pz in z_peers:
            z_copy(
                1, send_u.at[pl.ds(pl.multiple_of(pz * slots, slots), slots)],
                recv_u.at[pl.ds(pl.multiple_of(z * slots, slots), slots)], pz, z,
            ).start()
        chain_step(1, *b_args, b_value)
        tok_c.wait_recv()

        def pack_tile(cols):
            send_t[:, cols] = dot(pack_m[...], tok2[:, cols]).astype(BF16)

        tiled(dh, 512, pack_tile)
        my_slots = pl.ds(pl.multiple_of(z * slots, slots), slots)
        for pz in z_peers:
            z_copy(
                0, send_t.at[pl.ds(pl.multiple_of(pz * slots, slots), slots)], recv_t.at[my_slots], pz, z
            ).start()
        recv_t[my_slots, :] = send_t[my_slots, :]
        recv_u[my_slots, :] = send_u[my_slots, :]
        for s in range(2, b_steps):
            chain_step(s, *b_args, b_value)
        rows_all = pl.ds(0, er)
        bh[...] = (
            w_is * b_ref[:, my_vcols].astype(F32) + w_lt * load(b_r, rows_all) + w_gt * load(b_l, rows_all)
        ).astype(BF16)

        def rank_send(rnd, ref):
            for _, px, pc in xc_peers:
                pltpu.make_async_remote_copy(
                    ref.at[me_xc], ref.at[me_xc], rk_s.at[rnd, px * nc + pc], rk_r.at[rnd, me_xc],
                    device_id={"tensor": px, "dp": pc}, device_id_type=MESH,
                ).start()

        def rank_sum(rnd, ref):
            for o, px, pc in xc_peers:
                cp = pltpu.make_async_remote_copy(
                    ref.at[me_xc], ref.at[o], rk_s.at[rnd, o], rk_r.at[rnd, o],
                    device_id={"tensor": px, "dp": pc}, device_id_type=MESH,
                )
                cp.wait_recv()
                cp.wait_send()
            total = ref[0]
            for i in range(1, nx * nc):
                total += ref[i]
            return total

        def fold(full):
            return jnp.sum(full.reshape(e_local, ranks, full.shape[1]), axis=0)

        def spread(rank_rows, mask):
            rounded = rank_rows.astype(BF16).astype(F32)
            return jnp.concatenate([rounded] * e_local, axis=0) * mask

        rb_hot[me_xc] = fold(dot_nt(bh[...], u2[...]) * mask_h[...])
        rank_send(0, rb_hot)

        w_copy.wait()

        def base_tile(cols):
            basep[:, cols] = dot(tok_ref[...], w_ref[:, cols])

        tiled(v, 256, base_tile)
        for px in x_peers:
            pltpu.make_async_remote_copy(
                basep.at[:, pl.ds(pl.multiple_of(px * vl, vl), vl)], baser.at[x], bs_s.at[px], bs_r.at[x],
                device_id={"tensor": px}, device_id_type=MESH,
            ).start()

        s_back = spread(rank_sum(0, rb_hot), mask_h[...])
        spread_s[...] = s_back.astype(BF16)
        spread_t[...] = s_back.T.astype(BF16)

        def g_tile(cols):
            g_hot[:, cols] = SCALE * dot(spread_s[...], tok2[:, cols])

        tiled(dh, 512, g_tile)

        def c_value(way, rows, got):
            add = w_gt if way == 0 else w_lt
            return w_is * a_ref[rows, my_cols].astype(F32) + (1.0 - w_is) * got + add * g_hot[rows, :]

        c_args = (CHUNKS, c_r, c_l, c_sr, c_sl, cc_s, cc_r)

        def frozen_back():
            for px in x_peers:
                cp = pltpu.make_async_remote_copy(
                    u_ref, ufull.at[px], ux_s.at[px], ux_r.at[px], device_id={"tensor": px}, device_id_type=MESH
                )
                cp.wait_recv()
                cp.wait_send()
            up = jnp.concatenate([ufull[i] for i in range(nx)], axis=1)

            def tile(cols):
                fb[:, cols] = dot_nt(up, w_ref[cols, :])

            tiled(d, 512, tile)

        def rank_received():
            for pz in z_peers:
                ps = pl.ds(pl.multiple_of(pz * slots, slots), slots)
                for k, (src, dst) in enumerate(((send_t, recv_t), (send_u, recv_u))):
                    cp = z_copy(k, src.at[ps], dst.at[ps], pz, pz)
                    cp.wait_recv()
                    cp.wait_send()
            e_iota = lax.broadcasted_iota(jnp.int32, (er, 128), 0)
            j_iota = lax.broadcasted_iota(jnp.int32, (er, 128), 1) * ranks
            pick = jnp.where(e_iota >= j_iota, 1.0, 0.0) * jnp.where(e_iota < j_iota + ranks, 1.0, 0.0)
            mask_r[...] = dot_nt(pick.astype(BF16), recv_u[:, vh : vh + 128])
            rr[me_xc, 0:ranks, :] = fold(dot_nt(a_ref[:, my_cols], recv_t[...]) * mask_r[...])
            rr[me_xc, ranks : 2 * ranks, :] = fold(dot_nt(b_ref[:, my_vcols], recv_u[:, 0:vh]) * mask_r[...])
            rank_send(1, rr)

        def owner_work():
            both = rank_sum(1, rr)
            low = spread(both[0:ranks], mask_r[...])
            back = spread(both[ranks : 2 * ranks], mask_r[...])
            low_b, back_b = low.astype(BF16), back.astype(BF16)
            low_tr, back_tr = low.T.astype(BF16), back.T.astype(BF16)
            gu_ref[:, my_vcols] = SCALE * dot(low_b, recv_u[:, 0:vh])
            ret_u[...] = (SCALE * dot(low_tr, b_ref[:, my_vcols])).astype(BF16)
            for j in range(0, dh, 512):
                cols = pl.ds(j, 512)
                out_cols = pl.ds(pl.multiple_of(c * dh + j, 512), 512)
                gd_ref[:, out_cols] = SCALE * dot(back_b, recv_t[:, cols])
                ret_t[:, cols] = (SCALE * dot(back_tr, a_ref[:, out_cols])).astype(BF16)

        def send_returns():
            for pz in z_peers:
                ps = pl.ds(pl.multiple_of(pz * slots, slots), slots)
                z_copy(3, ret_u.at[ps], back_u.at[my_slots], pz, z).start()
                z_copy(2, ret_t.at[ps], back_t.at[my_slots], pz, z).start()
            back_t[my_slots, :] = ret_t[my_slots, :]
            back_u[my_slots, :] = ret_u[my_slots, :]

        c_steps = CHUNKS + n - 1
        hooks = {0: frozen_back, 4: rank_received, 6: owner_work, 7: send_returns}
        for s in range(c_steps):
            chain_step(s, *c_args, c_value)
            if s in hooks:
                hooks[s]()

        ah[...] = (
            w_is * a_ref[:, my_cols].astype(F32) + w_lt * load(c_r, rows_all) + w_gt * load(c_l, rows_all)
        ).astype(BF16)
        for j in range(0, t2, td):
            rl_hot[me_xc, :, j : j + td] = fold(dot_nt(ah[...], tok2[j : j + td, :]) * mask_h[:, j : j + td])
        rank_send(2, rl_hot)
        keep = 1.0 - w_is

        def gd_tile(i, carry):
            cols = pl.ds(pl.multiple_of(i * 512, 512), 512)
            out_cols = pl.ds(pl.multiple_of(c * dh + i * 512, 512), 512)
            total = g_hot[:, cols]
            for p in range(planes):
                total += c_r[p, :, cols].astype(F32) + c_l[p, :, cols].astype(F32)
            gd_ref[:, out_cols] = keep * gd_ref[:, out_cols] + w_is * total
            return carry

        lax.fori_loop(0, dh // 512, gd_tile, 0)
        gd_c = sib_copy(3, gd_ref.at[:, my_cols], gd_ref.at[:, my_cols])
        gd_c.start()

        low_s = spread(rank_sum(2, rl_hot), mask_h[...])
        low_b = low_s.astype(BF16)
        gv_hot[...] = SCALE * dot(low_b, u2[...])
        v_args = (SMALL_CHUNKS, v_r, v_l, v_sr, v_sl, vc_s, vc_r)

        def v_value(way, rows, got):
            return got + gv_hot[rows, :]

        chain_step(0, *v_args, v_value)

        def dx_tile(cols):
            dx2[:, cols] = (SCALE * dot(spread_t[...], ah[:, cols])).astype(BF16)

        tiled(dh, 512, dx_tile)
        chain_step(1, *v_args, v_value)
        lora_hot = (SCALE * dot(low_s.T.astype(BF16), bh[...])).astype(BF16).astype(F32)
        unpack = pack_m[...].astype(F32).T.astype(BF16)
        for s in range(2, SMALL_CHUNKS + n - 1):
            chain_step(s, *v_args, v_value)
        gu_ref[:, my_vcols] = keep * gu_ref[:, my_vcols] + w_is * (
            gv_hot[...] + load(v_r, rows_all) + load(v_l, rows_all)
        )
        gu_c = sib_copy(4, gu_ref.at[:, my_vcols], gu_ref.at[:, my_vcols])
        gu_c.start()

        for pz in z_peers:
            ps = pl.ds(pl.multiple_of(pz * slots, slots), slots)
            cp = z_copy(3, ret_u.at[ps], back_u.at[ps], pz, pz)
            cp.wait_recv()
            cp.wait_send()
        lo2[...] = (lora_hot + dot(unpack, back_u[...])).astype(BF16)
        lo_c = sib_copy(5, lo2.at[sib_rows], los)
        lo_c.start()
        for pz in z_peers:
            ps = pl.ds(pl.multiple_of(pz * slots, slots), slots)
            cp = z_copy(2, ret_t.at[ps], back_t.at[ps], pz, pz)
            cp.wait_recv()
            cp.wait_send()

        def un_tile(cols):
            dx2[:, cols] = (dx2[:, cols].astype(F32) + dot(unpack, back_t[:, cols])).astype(BF16)

        tiled(dh, 512, un_tile)
        dx_c = sib_copy(6, dx2.at[sib_rows], dxs)
        dx_c.start()

        for px in x_peers:
            cp = pltpu.make_async_remote_copy(
                basep.at[:, pl.ds(pl.multiple_of(px * vl, vl), vl)], baser.at[px], bs_s.at[px], bs_r.at[px],
                device_id={"tensor": px}, device_id_type=MESH,
            )
            cp.wait_recv()
            cp.wait_send()
        x_cols = pl.ds(pl.multiple_of(x * vl, vl), vl)
        baser[x] = basep[:, x_cols]
        frozen = baser[0]
        for i in range(1, nx):
            frozen += baser[i]
        basep[:, 0:vl] = frozen
        proj_ref[:, my_vcols] = (basep[:, my_vcols] + lo2[my_rows, :].astype(F32)).astype(BF16)
        dxo_ref[:, my_cols] = (fb[:, my_cols] + dx2[my_rows, :].astype(F32)).astype(BF16)
        lo_c.wait()
        proj_ref[:, sib_vcols] = (basep[:, sib_vcols] + los[...].astype(F32)).astype(BF16)
        dx_c.wait()
        dxo_ref[:, sib_cols] = (fb[:, sib_cols] + dxs[...].astype(F32)).astype(BF16)
        sib_copy(3, gd_ref.at[:, my_cols], gd_ref.at[:, sib_cols]).wait()
        sib_copy(4, gu_ref.at[:, my_vcols], gu_ref.at[:, sib_vcols]).wait()
        ta_c.wait_send()
        tok_c.wait_send()
        u_c.wait_send()
        chain_finish(*b_args)
        chain_finish(*c_args)
        chain_finish(*v_args)

    return kernel


def my_rows_of(c, td):
    return pl.ds(pl.multiple_of(c * td, td), td)


def shards(tokens, weight, down, up, token_adapter, storage_row, upstream):
    n, nx, nc = lax.axis_size("adapter"), lax.axis_size("tensor"), lax.axis_size("dp")
    td, d = tokens.shape
    e_local, ranks, vl = up.shape
    er, v = e_local * ranks, weight.shape[1]
    hot_load = 3 * td // n
    most = -(-(td - hot_load) // (n - 1))
    slots = -(-(nc * most) // 16) * 16
    planes = 1 if n <= 4 else 2
    dh, vh, t2, ns, xc = d // nc, vl // nc, nc * td, n * slots, nx * nc
    vm = pltpu.VMEM
    dma = pltpu.SemaphoreType.DMA
    scratch = [
        vm((d, v), BF16), vm((nc, 1, td), jnp.int32), vm((t2, dh), BF16), vm((t2, vh), BF16),
        vm((nx, td, vl), BF16), vm((td, v), F32), vm((nx, td, vl), F32), vm((td, d), F32),
        vm((ns, t2), BF16), vm((er, t2), F32), vm((er, ns), F32), vm((er, t2), BF16), vm((t2, er), BF16),
        vm((ns, dh), BF16), vm((ns, dh), BF16), vm((ns, vh + 128), BF16), vm((ns, vh + 128), BF16),
        vm((ns, dh), BF16), vm((ns, dh), BF16), vm((ns, vh), BF16), vm((ns, vh), BF16),
        vm((xc, ranks, t2), F32), vm((xc, ranks, t2), F32), vm((xc, 2 * ranks, ns), F32),
        *[vm((planes, er, vh), BF16)] * 4, vm((er, vh), BF16),
        *[vm((planes, er, dh), BF16)] * 4, vm((er, dh), F32), vm((er, dh), BF16),
        *[vm((planes, er, vh), BF16)] * 4, vm((er, vh), F32),
        vm((t2, dh), BF16), vm((td, dh), BF16), vm((t2, vh), BF16), vm((td, vh), BF16),
        dma, dma((2,)), dma((7,)), dma((7,)), dma((nx,)), dma((nx,)), dma((nx,)), dma((nx,)),
        dma((3, xc)), dma((3, xc)), dma((4, n)), dma((4, n)),
        dma((2, planes, SMALL_CHUNKS)), dma((2, planes, SMALL_CHUNKS)),
        dma((2, planes, CHUNKS)), dma((2, planes, CHUNKS)),
        dma((2, planes, SMALL_CHUNKS)), dma((2, planes, SMALL_CHUNKS)),
    ]
    vspec = pl.BlockSpec(memory_space=pltpu.VMEM)
    proj, dx, gd, gu = pl.pallas_call(
        make_kernel(n, nx, nc, ranks, slots, planes),
        out_shape=(
            jax.ShapeDtypeStruct((td, vl), BF16),
            jax.ShapeDtypeStruct((td, d), BF16),
            jax.ShapeDtypeStruct((er, d), F32),
            jax.ShapeDtypeStruct((er, vl), F32),
        ),
        in_specs=[vspec, vspec, vspec, pl.BlockSpec(memory_space=pl.ANY), vspec, vspec, vspec],
        out_specs=(vspec,) * 4,
        scratch_shapes=scratch,
        compiler_params=pltpu.CompilerParams(
            collective_id=0, has_side_effects=True, vmem_limit_bytes=60 * 1024 * 1024
        ),
        cost_estimate=pl.CostEstimate(flops=8_000_000_000, bytes_accessed=20_000_000, transcendentals=0),
    )(
        token_adapter.reshape(1, td), storage_row.reshape(1, -1), tokens, weight,
        down.reshape(er, d), up.reshape(er, vl), upstream,
    )
    return proj, dx, gd.reshape(e_local, ranks, d), gu.reshape(e_local, ranks, vl)


def solution(mesh):
    return jax.shard_map(
        shards,
        mesh=mesh,
        in_specs=(
            P(("groups", "adapter", "dp"), "tensor"),
            P("tensor", None),
            P(("groups", "adapter"), None, "tensor"),
            P(("groups", "adapter"), None, "tensor"),
            P(("groups", "adapter", "dp")),
            P("groups"),
            P(("groups", "adapter", "dp"), "tensor"),
        ),
        out_specs=(
            P(("groups", "adapter", "dp"), "tensor"),
            P(("groups", "adapter", "dp"), "tensor"),
            P(("groups", "adapter"), None, "tensor"),
            P(("groups", "adapter"), None, "tensor"),
        ),
        check_vma=False,
    )
```

```python
import jax
import jax.numpy as jnp
from jax import lax
from jax.experimental import pallas as pl
from jax.experimental.pallas import tpu as pltpu
from jax.sharding import PartitionSpec as P

MESH = pl.DeviceIdType.MESH
F32 = jnp.float32
BF16 = jnp.bfloat16
SCALE = 2.0
CHUNKS = 8
LAG = 2


def dot(a, b):
    return lax.dot_general(a, b, (((1,), (0,)), ((), ())), preferred_element_type=F32)


def dot_nt(a, b):
    return lax.dot_general(a, b, (((1,), (1,)), ((), ())), preferred_element_type=F32)


def tiled(total, tile, body):
    tile = min(tile, total)

    def step(i, carry):
        body(pl.ds(pl.multiple_of(i * tile, tile), tile))
        return carry

    lax.fori_loop(0, total // tile, step, 0)


def make_kernel(n, nx, nc, ranks, slots, planes):
    def kernel(
        ta_ref, asr_ref, tok_ref, w_hbm, a_ref, b_ref, u_ref,
        proj_ref, dxo_ref, gd_ref, gu_ref,
        w_ref, ta2, tok2, u2, ufull, basep, baser, fb,
        pack_m, mask_h, mask_r, spread_s, spread_t,
        send_t, recv_t, send_u, recv_u, ret_t, back_t, ret_u, back_u,
        rb_hot, rl_hot, rr,
        ball, bh,
        c_r, c_l, c_sr, c_sl, g_hot, ah,
        v_r, v_l, v_sr, v_sl, gv_hot,
        dx2, dxs, lo2, los,
        wsem, lsem, sib_s, sib_r, ux_s, ux_r, bs_s, bs_r, rk_s, rk_r, aa_s, aa_r,
        cc_s, cc_r, vc_s, vc_r,
    ):
        td, d = tok_ref.shape
        er = a_ref.shape[0]
        e_local = er // ranks
        vl = u_ref.shape[1]
        v = w_ref.shape[1]
        dh, vh = d // nc, vl // nc
        t2 = nc * td
        ns = n * slots
        z, x, c = lax.axis_index("adapter"), lax.axis_index("tensor"), lax.axis_index("dp")
        sib = lax.rem(c + 1, nc)
        me_xc = x * nc + c
        my_cols = pl.ds(pl.multiple_of(c * dh, dh), dh)
        sib_cols = pl.ds(pl.multiple_of(sib * dh, dh), dh)
        my_vcols = pl.ds(pl.multiple_of(c * vh, vh), vh)
        sib_vcols = pl.ds(pl.multiple_of(sib * vh, vh), vh)
        my_rows = pl.ds(pl.multiple_of(c * td, td), td)
        sib_rows = pl.ds(pl.multiple_of(sib * td, td), td)

        w_copy = pltpu.make_async_copy(w_hbm, w_ref, wsem)
        w_copy.start()

        xc_peers = []
        for j in range(1, nx * nc):
            o = lax.rem(me_xc + j, nx * nc)
            xc_peers.append((o, o // nc, o % nc))
        z_peers = [lax.rem(z + j, n) for j in range(1, n)]
        x_peers = [lax.rem(x + j, nx) for j in range(1, nx)]

        barrier = pltpu.get_barrier_semaphore()
        for _, px, pc in xc_peers:
            pl.semaphore_signal(barrier, inc=1, device_id={"tensor": px, "dp": pc}, device_id_type=MESH)
        for pz in z_peers:
            pl.semaphore_signal(barrier, inc=1, device_id={"adapter": pz}, device_id_type=MESH)
        pl.semaphore_wait(barrier, len(xc_peers) + len(z_peers))

        def sib_copy(k, src, dst):
            return pltpu.make_async_remote_copy(
                src, dst, sib_s.at[k], sib_r.at[k], device_id={"dp": sib}, device_id_type=MESH
            )

        def z_copy(k, src, dst, to, frm):
            return pltpu.make_async_remote_copy(
                src, dst, aa_s.at[k, to], aa_r.at[k, frm], device_id={"adapter": to}, device_id_type=MESH
            )

        ta_c = sib_copy(0, ta_ref, ta2.at[c])
        tok_c = sib_copy(1, tok_ref.at[:, sib_cols], tok2.at[my_rows])
        u_c = sib_copy(2, u_ref.at[:, sib_vcols], u2.at[my_rows])
        for pz in z_peers:
            z_copy(4, b_ref.at[:, my_vcols], ball.at[z], pz, z).start()
        ball[z] = b_ref[:, my_vcols]
        ta_c.start()
        u_c.start()
        tok_c.start()
        for px in x_peers:
            pltpu.make_async_remote_copy(
                u_ref, ufull.at[x], ux_s.at[px], ux_r.at[x], device_id={"tensor": px}, device_id_type=MESH
            ).start()
        tok_l = pltpu.make_async_copy(tok_ref.at[:, my_cols], tok2.at[my_rows_of(c, td)], lsem.at[0])
        u_l = pltpu.make_async_copy(u_ref.at[:, my_vcols], u2.at[my_rows_of(c, td)], lsem.at[1])
        tok_l.start()
        u_l.start()
        ta2[c] = ta_ref[...]
        ufull[x] = u_ref[...]

        ta_c.wait_recv()
        ids = jnp.concatenate([ta2[i] for i in range(nc)], axis=1)
        at = asr_ref.shape[1]
        match = (lax.broadcasted_iota(jnp.int32, (at, t2), 0) == ids).astype(F32).astype(BF16)
        table = jnp.broadcast_to(asr_ref[...].astype(F32), (8, at)).astype(BF16)
        storage = dot(table, match)[0:1, :]
        owner = jnp.floor(storage * (1.0 / e_local))
        slot = storage - owner * e_local
        n8 = max(8, n)
        own_iota = lax.broadcasted_iota(jnp.int32, (n8, t2), 0).astype(F32)
        own_hit = jnp.where(own_iota == owner, 1.0, 0.0)
        loads = jnp.sum(own_hit, axis=1, keepdims=True)
        top = jnp.max(loads)
        hot = jnp.sum(jnp.where(loads == top, lax.broadcasted_iota(jnp.int32, (n8, 1), 0).astype(F32), 0.0))
        zf = z.astype(F32)
        w_is = jnp.where(hot == zf, 1.0, 0.0)
        w_lt = jnp.where(hot < zf, 1.0, 0.0)
        w_gt = jnp.where(hot > zf, 1.0, 0.0)
        tri = (
            lax.broadcasted_iota(jnp.int32, (t2, t2), 0) < lax.broadcasted_iota(jnp.int32, (t2, t2), 1)
        ).astype(F32).astype(BF16)
        pos = jnp.sum(dot(own_hit.astype(BF16), tri) * own_hit, axis=0, keepdims=True)
        target = jnp.where(owner == hot, -1.0, owner * slots + pos)
        pack_m[...] = jnp.where(
            lax.broadcasted_iota(jnp.int32, (ns, t2), 0).astype(F32) == target, 1.0, 0.0
        ).astype(BF16)
        begin = jnp.where(owner == hot, slot * ranks, -1.0 * ranks)
        er_iota = lax.broadcasted_iota(jnp.int32, (er, t2), 0).astype(F32)
        mask_h[...] = jnp.where(er_iota >= begin, 1.0, 0.0) * jnp.where(er_iota < begin + ranks, 1.0, 0.0)
        slot_hit = jnp.where(
            lax.broadcasted_iota(jnp.int32, (128, t2), 0).astype(F32) == slot, 1.0, 0.0
        ).astype(BF16)

        def clear_edges(right, left):
            @pl.when(z == 0)
            def _():
                right[...] = jnp.zeros_like(right)

            @pl.when(z == n - 1)
            def _():
                left[...] = jnp.zeros_like(left)

        def load(ref, rows):
            total = ref[0, rows, :].astype(F32)
            for p in range(1, planes):
                total += ref[p, rows, :].astype(F32)
            return total

        def store(ref, rows, value):
            for p in range(planes):
                part = value.astype(BF16)
                ref[p, rows, :] = part
                value = value - part.astype(F32)

        def chain_copy(src, dst, ssem, rsem, way, k, rows, to):
            return [
                pltpu.make_async_remote_copy(
                    src.at[p, rows], dst.at[p, rows], ssem.at[way, p, k], rsem.at[way, p, k],
                    device_id={"adapter": to}, device_id_type=MESH,
                )
                for p in range(planes)
            ]

        def chain_step(s, chunks, lag_by, rr_, rl_, sr_, sl_, ssem, rsem, value):
            rc = er // chunks
            for way, (rin, sout, lag, edge_in, edge_out, step) in enumerate((
                (rr_, sr_, lag_by * z, z == 0, z == n - 1, 1),
                (rl_, sl_, lag_by * (n - 1 - z), z == n - 1, z == 0, -1),
            )):
                k = s - lag

                @pl.when(jnp.logical_and(k >= 0, k < chunks))
                def _():
                    rows = pl.ds(pl.multiple_of(k * rc, rc), rc)
                    to = lax.rem(z + step + n, n)

                    @pl.when(jnp.logical_not(edge_in))
                    def _():
                        for cp in chain_copy(sout, rin, ssem, rsem, way, k, rows, to):
                            cp.wait_recv()

                    @pl.when(jnp.logical_not(edge_out))
                    def _():
                        store(sout, rows, value(way, rows, load(rin, rows)))
                        for cp in chain_copy(sout, rin, ssem, rsem, way, k, rows, to):
                            cp.start()

        def chain_finish(chunks, lag_by, rr_, rl_, sr_, sl_, ssem, rsem):
            rc = er // chunks
            for way, (rin, sout, edge_out, step) in enumerate(
                ((rr_, sr_, z == n - 1, 1), (rl_, sl_, z == 0, -1))
            ):
                to = lax.rem(z + step + n, n)

                @pl.when(jnp.logical_not(edge_out))
                def _():
                    for k in range(chunks):
                        for cp in chain_copy(sout, rin, ssem, rsem, way, k, pl.ds(k * rc, rc), to):
                            cp.wait_send()

        clear_edges(c_r, c_l)
        clear_edges(v_r, v_l)

        tok_l.wait()
        u_l.wait()
        u_c.wait_recv()
        send_u[:, 0:vh] = dot(pack_m[...], u2[...]).astype(BF16)
        send_u[:, vh : vh + 128] = dot_nt(pack_m[...], slot_hit).astype(BF16)
        for pz in z_peers:
            z_copy(
                1, send_u.at[pl.ds(pl.multiple_of(pz * slots, slots), slots)],
                recv_u.at[pl.ds(pl.multiple_of(z * slots, slots), slots)], pz, z,
            ).start()
        tok_c.wait_recv()

        def pack_tile(cols):
            send_t[:, cols] = dot(pack_m[...], tok2[:, cols]).astype(BF16)

        tiled(dh, 512, pack_tile)
        my_slots = pl.ds(pl.multiple_of(z * slots, slots), slots)
        for pz in z_peers:
            z_copy(
                0, send_t.at[pl.ds(pl.multiple_of(pz * slots, slots), slots)], recv_t.at[my_slots], pz, z
            ).start()
        recv_t[my_slots, :] = send_t[my_slots, :]
        recv_u[my_slots, :] = send_u[my_slots, :]
        for pz in z_peers:
            cp = z_copy(4, b_ref.at[:, my_vcols], ball.at[pz], pz, pz)
            cp.wait_recv()
            cp.wait_send()
        rows_all = pl.ds(0, er)
        hot_up = jnp.zeros((er, vh), F32)
        for i in range(n):
            hot_up += jnp.where(hot == i, 1.0, 0.0) * ball[i].astype(F32)
        bh[...] = hot_up.astype(BF16)

        def rank_send(rnd, ref):
            for _, px, pc in xc_peers:
                pltpu.make_async_remote_copy(
                    ref.at[me_xc], ref.at[me_xc], rk_s.at[rnd, px * nc + pc], rk_r.at[rnd, me_xc],
                    device_id={"tensor": px, "dp": pc}, device_id_type=MESH,
                ).start()

        def rank_sum(rnd, ref):
            for o, px, pc in xc_peers:
                cp = pltpu.make_async_remote_copy(
                    ref.at[me_xc], ref.at[o], rk_s.at[rnd, o], rk_r.at[rnd, o],
                    device_id={"tensor": px, "dp": pc}, device_id_type=MESH,
                )
                cp.wait_recv()
                cp.wait_send()
            total = ref[0]
            for i in range(1, nx * nc):
                total += ref[i]
            return total

        def fold(full):
            return jnp.sum(full.reshape(e_local, ranks, full.shape[1]), axis=0)

        def spread(rank_rows, mask):
            rounded = rank_rows.astype(BF16).astype(F32)
            return jnp.concatenate([rounded] * e_local, axis=0) * mask

        rb_hot[me_xc] = fold(dot_nt(bh[...], u2[...]) * mask_h[...])
        rank_send(0, rb_hot)

        w_copy.wait()

        def base_tile(cols):
            basep[:, cols] = dot(tok_ref[...], w_ref[:, cols])

        tiled(v, 256, base_tile)
        for px in x_peers:
            pltpu.make_async_remote_copy(
                basep.at[:, pl.ds(pl.multiple_of(px * vl, vl), vl)], baser.at[x], bs_s.at[px], bs_r.at[x],
                device_id={"tensor": px}, device_id_type=MESH,
            ).start()

        s_back = spread(rank_sum(0, rb_hot), mask_h[...])
        spread_s[...] = s_back.astype(BF16)
        spread_t[...] = s_back.T.astype(BF16)

        def g_tile(cols):
            g_hot[:, cols] = SCALE * dot(spread_s[...], tok2[:, cols])

        tiled(dh, 512, g_tile)

        def c_value(way, rows, got):
            add = w_gt if way == 0 else w_lt
            return w_is * a_ref[rows, my_cols].astype(F32) + (1.0 - w_is) * got + add * g_hot[rows, :]

        c_args = (CHUNKS, LAG, c_r, c_l, c_sr, c_sl, cc_s, cc_r)

        def frozen_back():
            for px in x_peers:
                cp = pltpu.make_async_remote_copy(
                    u_ref, ufull.at[px], ux_s.at[px], ux_r.at[px], device_id={"tensor": px}, device_id_type=MESH
                )
                cp.wait_recv()
                cp.wait_send()
            up = jnp.concatenate([ufull[i] for i in range(nx)], axis=1)

            def tile(cols):
                fb[:, cols] = dot_nt(up, w_ref[cols, :])

            tiled(d, 512, tile)

        def rank_received():
            for pz in z_peers:
                ps = pl.ds(pl.multiple_of(pz * slots, slots), slots)
                for k, (src, dst) in enumerate(((send_t, recv_t), (send_u, recv_u))):
                    cp = z_copy(k, src.at[ps], dst.at[ps], pz, pz)
                    cp.wait_recv()
                    cp.wait_send()
            e_iota = lax.broadcasted_iota(jnp.int32, (er, 128), 0)
            j_iota = lax.broadcasted_iota(jnp.int32, (er, 128), 1) * ranks
            pick = jnp.where(e_iota >= j_iota, 1.0, 0.0) * jnp.where(e_iota < j_iota + ranks, 1.0, 0.0)
            mask_r[...] = dot_nt(pick.astype(BF16), recv_u[:, vh : vh + 128])
            rr[me_xc, 0:ranks, :] = fold(dot_nt(a_ref[:, my_cols], recv_t[...]) * mask_r[...])
            rr[me_xc, ranks : 2 * ranks, :] = fold(dot_nt(b_ref[:, my_vcols], recv_u[:, 0:vh]) * mask_r[...])
            rank_send(1, rr)

        def owner_work():
            both = rank_sum(1, rr)
            low = spread(both[0:ranks], mask_r[...])
            back = spread(both[ranks : 2 * ranks], mask_r[...])
            low_b, back_b = low.astype(BF16), back.astype(BF16)
            low_tr, back_tr = low.T.astype(BF16), back.T.astype(BF16)
            gu_ref[:, my_vcols] = SCALE * dot(low_b, recv_u[:, 0:vh])
            ret_u[...] = (SCALE * dot(low_tr, b_ref[:, my_vcols])).astype(BF16)
            for j in range(0, dh, 512):
                cols = pl.ds(j, 512)
                out_cols = pl.ds(pl.multiple_of(c * dh + j, 512), 512)
                gd_ref[:, out_cols] = SCALE * dot(back_b, recv_t[:, cols])
                ret_t[:, cols] = (SCALE * dot(back_tr, a_ref[:, out_cols])).astype(BF16)

        def send_returns():
            for pz in z_peers:
                ps = pl.ds(pl.multiple_of(pz * slots, slots), slots)
                z_copy(3, ret_u.at[ps], back_u.at[my_slots], pz, z).start()
                z_copy(2, ret_t.at[ps], back_t.at[my_slots], pz, z).start()
            back_t[my_slots, :] = ret_t[my_slots, :]
            back_u[my_slots, :] = ret_u[my_slots, :]

        c_steps = CHUNKS + LAG * (n - 1)
        hooks = {0: frozen_back, 7: rank_received, 10: owner_work, 13: send_returns}
        for s in range(c_steps):
            chain_step(s, *c_args, c_value)
            if s in hooks:
                hooks[s]()

        ah[...] = (
            w_is * a_ref[:, my_cols].astype(F32) + w_lt * load(c_r, rows_all) + w_gt * load(c_l, rows_all)
        ).astype(BF16)
        for j in range(0, t2, td):
            rl_hot[me_xc, :, j : j + td] = fold(dot_nt(ah[...], tok2[j : j + td, :]) * mask_h[:, j : j + td])
        rank_send(2, rl_hot)
        keep = 1.0 - w_is

        def gd_tile(i, carry):
            cols = pl.ds(pl.multiple_of(i * 512, 512), 512)
            out_cols = pl.ds(pl.multiple_of(c * dh + i * 512, 512), 512)
            total = g_hot[:, cols]
            for p in range(planes):
                total += c_r[p, :, cols].astype(F32) + c_l[p, :, cols].astype(F32)
            gd_ref[:, out_cols] = keep * gd_ref[:, out_cols] + w_is * total
            return carry

        lax.fori_loop(0, dh // 512, gd_tile, 0)
        gd_c = sib_copy(3, gd_ref.at[:, my_cols], gd_ref.at[:, my_cols])
        gd_c.start()

        low_s = spread(rank_sum(2, rl_hot), mask_h[...])
        low_b = low_s.astype(BF16)
        gv_hot[...] = SCALE * dot(low_b, u2[...])
        v_args = (1, 1, v_r, v_l, v_sr, v_sl, vc_s, vc_r)

        def v_value(way, rows, got):
            return got + gv_hot[rows, :]

        chain_step(0, *v_args, v_value)

        def dx_tile(cols):
            dx2[:, cols] = (SCALE * dot(spread_t[...], ah[:, cols])).astype(BF16)

        tiled(dh, 512, dx_tile)
        chain_step(1, *v_args, v_value)
        lora_hot = (SCALE * dot(low_s.T.astype(BF16), bh[...])).astype(BF16).astype(F32)
        unpack = pack_m[...].astype(F32).T.astype(BF16)
        for pz in z_peers:
            ps = pl.ds(pl.multiple_of(pz * slots, slots), slots)
            cp = z_copy(3, ret_u.at[ps], back_u.at[ps], pz, pz)
            cp.wait_recv()
            cp.wait_send()
        lo2[...] = (lora_hot + dot(unpack, back_u[...])).astype(BF16)
        lo_c = sib_copy(5, lo2.at[sib_rows], los)
        lo_c.start()
        chain_step(2, *v_args, v_value)
        for pz in z_peers:
            ps = pl.ds(pl.multiple_of(pz * slots, slots), slots)
            cp = z_copy(2, ret_t.at[ps], back_t.at[ps], pz, pz)
            cp.wait_recv()
            cp.wait_send()

        def un_tile(cols):
            dx2[:, cols] = (dx2[:, cols].astype(F32) + dot(unpack, back_t[:, cols])).astype(BF16)

        tiled(dh, 512, un_tile)
        dx_c = sib_copy(6, dx2.at[sib_rows], dxs)
        dx_c.start()
        for s in range(3, n):
            chain_step(s, *v_args, v_value)
        gu_ref[:, my_vcols] = keep * gu_ref[:, my_vcols] + w_is * (
            gv_hot[...] + load(v_r, rows_all) + load(v_l, rows_all)
        )
        gu_c = sib_copy(4, gu_ref.at[:, my_vcols], gu_ref.at[:, my_vcols])
        gu_c.start()

        for px in x_peers:
            cp = pltpu.make_async_remote_copy(
                basep.at[:, pl.ds(pl.multiple_of(px * vl, vl), vl)], baser.at[px], bs_s.at[px], bs_r.at[px],
                device_id={"tensor": px}, device_id_type=MESH,
            )
            cp.wait_recv()
            cp.wait_send()
        x_cols = pl.ds(pl.multiple_of(x * vl, vl), vl)
        baser[x] = basep[:, x_cols]
        frozen = baser[0]
        for i in range(1, nx):
            frozen += baser[i]
        basep[:, 0:vl] = frozen
        proj_ref[:, my_vcols] = (basep[:, my_vcols] + lo2[my_rows, :].astype(F32)).astype(BF16)
        dxo_ref[:, my_cols] = (fb[:, my_cols] + dx2[my_rows, :].astype(F32)).astype(BF16)
        lo_c.wait()
        proj_ref[:, sib_vcols] = (basep[:, sib_vcols] + los[...].astype(F32)).astype(BF16)
        dx_c.wait()
        dxo_ref[:, sib_cols] = (fb[:, sib_cols] + dxs[...].astype(F32)).astype(BF16)
        sib_copy(3, gd_ref.at[:, my_cols], gd_ref.at[:, sib_cols]).wait()
        sib_copy(4, gu_ref.at[:, my_vcols], gu_ref.at[:, sib_vcols]).wait()
        ta_c.wait_send()
        tok_c.wait_send()
        u_c.wait_send()
        chain_finish(*c_args)
        chain_finish(*v_args)

    return kernel


def my_rows_of(c, td):
    return pl.ds(pl.multiple_of(c * td, td), td)


def shards(tokens, weight, down, up, token_adapter, storage_row, upstream):
    n, nx, nc = lax.axis_size("adapter"), lax.axis_size("tensor"), lax.axis_size("dp")
    td, d = tokens.shape
    e_local, ranks, vl = up.shape
    er, v = e_local * ranks, weight.shape[1]
    hot_load = 3 * td // n
    most = -(-(td - hot_load) // (n - 1))
    slots = -(-(nc * most) // 16) * 16
    planes = 1 if n <= 4 else 2
    dh, vh, t2, ns, xc = d // nc, vl // nc, nc * td, n * slots, nx * nc
    vm = pltpu.VMEM
    dma = pltpu.SemaphoreType.DMA
    scratch = [
        vm((d, v), BF16), vm((nc, 1, td), jnp.int32), vm((t2, dh), BF16), vm((t2, vh), BF16),
        vm((nx, td, vl), BF16), vm((td, v), F32), vm((nx, td, vl), F32), vm((td, d), F32),
        vm((ns, t2), BF16), vm((er, t2), F32), vm((er, ns), F32), vm((er, t2), BF16), vm((t2, er), BF16),
        vm((ns, dh), BF16), vm((ns, dh), BF16), vm((ns, vh + 128), BF16), vm((ns, vh + 128), BF16),
        vm((ns, dh), BF16), vm((ns, dh), BF16), vm((ns, vh), BF16), vm((ns, vh), BF16),
        vm((xc, ranks, t2), F32), vm((xc, ranks, t2), F32), vm((xc, 2 * ranks, ns), F32),
        vm((n, er, vh), BF16), vm((er, vh), BF16),
        *[vm((planes, er, dh), BF16)] * 4, vm((er, dh), F32), vm((er, dh), BF16),
        *[vm((planes, er, vh), BF16)] * 4, vm((er, vh), F32),
        vm((t2, dh), BF16), vm((td, dh), BF16), vm((t2, vh), BF16), vm((td, vh), BF16),
        dma, dma((2,)), dma((7,)), dma((7,)), dma((nx,)), dma((nx,)), dma((nx,)), dma((nx,)),
        dma((3, xc)), dma((3, xc)), dma((5, n)), dma((5, n)),
        dma((2, planes, CHUNKS)), dma((2, planes, CHUNKS)), dma((2, planes, 1)), dma((2, planes, 1)),
    ]
    vspec = pl.BlockSpec(memory_space=pltpu.VMEM)
    proj, dx, gd, gu = pl.pallas_call(
        make_kernel(n, nx, nc, ranks, slots, planes),
        out_shape=(
            jax.ShapeDtypeStruct((td, vl), BF16),
            jax.ShapeDtypeStruct((td, d), BF16),
            jax.ShapeDtypeStruct((er, d), F32),
            jax.ShapeDtypeStruct((er, vl), F32),
        ),
        in_specs=[vspec, vspec, vspec, pl.BlockSpec(memory_space=pl.ANY), vspec, vspec, vspec],
        out_specs=(vspec,) * 4,
        scratch_shapes=scratch,
        compiler_params=pltpu.CompilerParams(
            collective_id=0, has_side_effects=True, vmem_limit_bytes=60 * 1024 * 1024
        ),
        cost_estimate=pl.CostEstimate(flops=8_000_000_000, bytes_accessed=20_000_000, transcendentals=0),
    )(
        token_adapter.reshape(1, td), storage_row.reshape(1, -1), tokens, weight,
        down.reshape(er, d), up.reshape(er, vl), upstream,
    )
    return proj, dx, gd.reshape(e_local, ranks, d), gu.reshape(e_local, ranks, vl)


def solution(mesh):
    return jax.shard_map(
        shards,
        mesh=mesh,
        in_specs=(
            P(("groups", "adapter", "dp"), "tensor"),
            P("tensor", None),
            P(("groups", "adapter"), None, "tensor"),
            P(("groups", "adapter"), None, "tensor"),
            P(("groups", "adapter", "dp")),
            P("groups"),
            P(("groups", "adapter", "dp"), "tensor"),
        ),
        out_specs=(
            P(("groups", "adapter", "dp"), "tensor"),
            P(("groups", "adapter", "dp"), "tensor"),
            P(("groups", "adapter"), None, "tensor"),
            P(("groups", "adapter"), None, "tensor"),
        ),
        check_vma=False,
    )
```
